32 devices in a mesh: rep: 8 (over z, x), shard: 4 (over y, core).
Axes of the slice: x: 2, y: 2, z: 4, core: 2. Of those that a mesh axis runs over, the one named last changes fastest.
Arguments:
- hidden_in: bfloat16 [32768, 768], P(('rep', 'shard')), may hold values from -6 to 6
- segment_ids: int32 [32768], P(('rep', 'shard')), may hold values from -1 to 127, as said below
- cotangent: bfloat16 [32768, 768], P(('rep', 'shard')), may hold values from -6 to 6
- ln1_gain: bfloat16 [768], P('shard'), may hold values from 0.5 to 1.5
- ln1_bias: bfloat16 [768], P('shard'), may hold values from -1.5 to 1.5
- ln2_gain: bfloat16 [768], P('shard'), may hold values from 0.5 to 1.5
- ln2_bias: bfloat16 [768], P('shard'), may hold values from -1.5 to 1.5
- qkv_weight: bfloat16 [768, 2304], P('shard'), may hold values from -0.21875 to 0.21875
- qkv_bias: bfloat16 [2304], P('shard'), may hold values from -1.5 to 1.5
- out_weight: bfloat16 [768, 768], P('shard'), may hold values from -0.875 to 0.875
- out_bias: bfloat16 [768], P('shard'), may hold values from -1.5 to 1.5
- up_weight: bfloat16 [768, 3072], P('shard'), may hold values from -0.21875 to 0.21875
- up_bias: bfloat16 [3072], P('shard'), may hold values from -2.5 to 2.5
- down_weight: bfloat16 [3072, 768], P('shard'), may hold values from -0.109375 to 0.109375
- down_bias: bfloat16 [768], P('shard'), may hold values from -1.5 to 1.5
Outputs:
- mixed: bfloat16 [32768, 768], P(('rep', 'shard'))
- input_grad: float32 [32768, 768], P(('rep', 'shard'))
- grad_ln1_gain: float32 [768], P('shard')
- grad_ln1_bias: float32 [768], P('shard')
- grad_ln2_gain: float32 [768], P('shard')
- grad_ln2_bias: float32 [768], P('shard')
- grad_qkv_weight: float32 [768, 2304], P('shard')
- grad_qkv_bias: float32 [2304], P('shard')
- grad_out_weight: float32 [768, 768], P('shard')
- grad_out_bias: float32 [768], P('shard')
- grad_up_weight: float32 [768, 3072], P('shard')
- grad_up_bias: float32 [3072], P('shard')
- grad_down_weight: float32 [3072, 768], P('shard')
- grad_down_bias: float32 [768], P('shard')
The draws below stay inside these ranges and needn't reach their ends.
Inputs may be any that keep to these rules, and one draw needn't show every extreme that they name: `segment_ids`: A sequence is a run of slots with one id 0 or more; its slots are consecutive, lie within one device's 1024 slots and number at most 1024; ids differ between sequences and rise along the slots; -1 marks unused slots, which come after a device's sequences; every device uses at least half of its slots, and some device holds a sequence of exactly 1024 slots.
All inputs are finite; a program needn't handle non-finite values.
Results may differ from the reference program's by a relative error of at most 0.0093.
Values may be sent and summed in bfloat16 or wider, within the bound.
A program may use at most 192 MiB of HBM per device.

```python
import jax
import jax.numpy as jnp
from jax import lax

D = 768
HEADS = 12
HEAD_DIM = 64
FF = 3072
ROTARY = 16
LONGEST = 1024
TOK_DEV = 1024
TOKENS = 32768


def draw_segment_ids(key, part):
    key = jax.random.fold_in(key, 11)
    block_count = TOKENS // TOK_DEV
    stride = TOK_DEV // LONGEST + 3
    chosen = jax.random.randint(jax.random.fold_in(key, 1), (), 0, block_count)
    filled = jax.random.randint(jax.random.fold_in(key, 2), (block_count,), TOK_DEV // 2, TOK_DEV)
    upper = jnp.maximum(filled, 2)
    cut_points = jax.random.randint(jax.random.fold_in(key, 3), (block_count, 3), 1, upper[:, None])
    late_cuts = LONGEST + jax.random.randint(jax.random.fold_in(key, 4), (block_count, 3), 0, max(TOK_DEV - LONGEST, 1))
    is_chosen = jnp.arange(block_count) == chosen
    cut_points = jnp.where(is_chosen[:, None], late_cuts, cut_points)
    filled = jnp.where(is_chosen, TOK_DEV, filled)
    slot_index = jnp.arange(TOK_DEV)
    local_ids = slot_index[None, :] // LONGEST + jnp.sum((cut_points[:, :, None] <= slot_index[None, None, :]).astype(jnp.int32), 1)
    last_slot = (filled - 1).astype(jnp.int32)
    last_local = jnp.take_along_axis(local_ids, last_slot[:, None], axis=1)
    global_ids = jnp.arange(block_count)[:, None] * stride + (stride - 1) - (last_local - local_ids)
    global_ids = jnp.where(slot_index[None, :] < filled[:, None], global_ids, -1)
    return global_ids.reshape(TOKENS).astype(jnp.int32)


def shard_levels(key, shape, pieces, low, largest):
    level = 1.0
    for dim, shards_of in pieces:
        steps = jax.random.uniform(jax.random.fold_in(jax.random.fold_in(key, 6), dim), (shards_of,), jnp.float32, low / len(pieces), largest / len(pieces))
        level = level * jnp.repeat(jnp.exp(steps), shape[dim] // shards_of).reshape((-1,) + (1,) * (len(shape) - 1 - dim))
    return level


def scatter_about(key, extent, scale, reach, shards=(), kind=jnp.bfloat16):
    level = shard_levels(key, extent, shards, -0.22, 0.18) if shards else 1.0
    entries = jax.random.normal(key, extent, jnp.float32) * scale * level
    return jnp.minimum(jnp.maximum(entries, -reach), reach).astype(kind)


def setup_inputs(seed: int = 0) -> dict:
    key_list = jax.random.split(jax.random.key(seed), 16)
    return {
        "hidden_in": scatter_about(key_list[0], (TOKENS, D), 1.0, 6.0, ((0, 32),)),
        "segment_ids": draw_segment_ids(jax.random.fold_in(key_list[15], 71), 0),
        "cotangent": scatter_about(key_list[2], (TOKENS, D), 1.0, 6.0, ((0, 32),)),
        "ln1_gain": jnp.clip(1.0 + 0.1 * jax.random.normal(key_list[3], (D,), jnp.float32), 0.5, 1.5).astype(jnp.bfloat16),
        "ln1_bias": scatter_about(key_list[4], (D,), 0.3, 1.5, ((0, 4),)),
        "ln2_gain": jnp.clip(1.0 + 0.1 * jax.random.normal(key_list[5], (D,), jnp.float32), 0.5, 1.5).astype(jnp.bfloat16),
        "ln2_bias": scatter_about(key_list[6], (D,), 0.3, 1.5, ((0, 4),)),
        "qkv_weight": scatter_about(key_list[7], (D, 3 * D), D ** -0.5, 0.21875, ((0, 4),)),
        "qkv_bias": scatter_about(key_list[8], (3 * D,), 0.3, 1.5, ((0, 4),)),
        "out_weight": scatter_about(key_list[9], (D, D), (D // 16) ** -0.5, 0.875, ((0, 4),)),
        "out_bias": scatter_about(key_list[10], (D,), 0.3, 1.5, ((0, 4),)),
        "up_weight": scatter_about(key_list[11], (D, FF), D ** -0.5, 0.21875, ((0, 4),)),
        "up_bias": scatter_about(key_list[12], (FF,), 0.5, 2.5, ((0, 4),)),
        "down_weight": scatter_about(key_list[13], (FF, D), FF ** -0.5, 0.109375, ((0, 4),)),
        "down_bias": scatter_about(key_list[14], (D,), 0.3, 1.5, ((0, 4),)),
    }


@jax.custom_vjp
def low(v):
    return lax.optimization_barrier(v.astype(jnp.bfloat16)).astype(jnp.float32)

@jax.custom_vjp
def low_back(v):
    return v

def low_keep(v):
    return (low(v), None)

def low_pass(kept, grad):
    return (grad,)

def back_keep(v):
    return (v, None)

def back_low(kept, grad):
    return (low(grad),)
low.defvjp(low_keep, low_pass)
low_back.defvjp(back_keep, back_low)
EPS = 1e-05
HIGH = lax.Precision.HIGHEST

def product(left, right):
    return jnp.dot(left, right, precision=HIGH)

def layer_norm(values, gain, bias):
    center = values - lax.optimization_barrier(jnp.mean(values, -1, keepdims=True))
    spread = lax.optimization_barrier(jnp.mean(center * center, -1, keepdims=True))
    return center * lax.rsqrt(spread + EPS) * gain + bias

def positions(segments):
    slot_index = jnp.arange(segments.shape[0], dtype=jnp.int32)
    is_start = jnp.concatenate([jnp.ones((1,), bool), segments[1:] != segments[:-1]])
    seq_start = lax.cummax(jnp.where(is_start, slot_index, jnp.zeros_like(slot_index)), axis=0)
    return slot_index - seq_start

def angles(places):
    rates = 10000.0 ** (-(jnp.arange(ROTARY // 2, dtype=jnp.float32) * 2.0) / ROTARY)
    turned = places.astype(jnp.float32)[:, None] * rates[None, :]
    turned = jnp.concatenate([turned, turned], -1)
    return (jnp.cos(turned)[:, None, :], jnp.sin(turned)[:, None, :])

def rotate(heads_in, cosine, sine_table):
    front = heads_in[..., :ROTARY]
    half = ROTARY // 2
    swapped = jnp.concatenate([-front[..., half:], front[..., :half]], -1)
    return jnp.concatenate([front * cosine + swapped * sine_table, heads_in[..., ROTARY:]], -1)

def layer(block_x, block_seg, params):
    gain_one, bias_one, gain_two, bias_two, w_qkv, b_qkv, w_out, b_out, w_up, b_up, w_down, b_down = params
    length = block_x.shape[0]
    first_in = low(layer_norm(block_x, gain_one, bias_one))
    qkv = low_back(product(first_in, w_qkv) + b_qkv)
    cosine, sine_table = angles(positions(block_seg))
    split = qkv.reshape(length, 3, HEADS, HEAD_DIM)
    query_rows = low(rotate(split[:, 0], cosine, sine_table))
    key_rows = low(rotate(split[:, 1], cosine, sine_table))
    value_rows = low(split[:, 2])
    raw = low_back(jnp.einsum('qhd,khd->hqk', query_rows, key_rows, precision=HIGH) * 0.125)
    slot_index = jnp.arange(length)
    readable = (block_seg[:, None] == block_seg[None, :]) & (slot_index[:, None] >= slot_index[None, :])
    scores = jnp.where(readable[None], raw, -1e+30)
    weights = low(jax.nn.softmax(scores, axis=-1))
    mixed_heads = jnp.einsum('hqk,khd->qhd', weights, value_rows, precision=HIGH).reshape(length, D)
    attended = low_back(low(mixed_heads))
    attn = product(attended, w_out) + b_out
    second_in = low(layer_norm(block_x, gain_two, bias_two))
    upward = low_back(product(second_in, w_up) + b_up)
    active = low(jax.nn.gelu(upward, approximate=False))
    feed = product(active, w_down) + b_down
    return block_x + attn + feed

def forward(x_all, segments, params):
    blocks = x_all.reshape(-1, TOK_DEV, D)
    seg_blocks = segments.reshape(-1, TOK_DEV)
    run_block = jax.checkpoint(lambda block_x, block_seg: layer(block_x, block_seg, params))

    def advance(running, inputs):
        return (running, run_block(inputs[0], inputs[1]))
    _, outputs = lax.scan(advance, jnp.zeros((), jnp.float32), (blocks, seg_blocks))
    return outputs.reshape(-1, D)

def reference(hidden_in, segment_ids, cotangent, ln1_gain, ln1_bias, ln2_gain, ln2_bias, qkv_weight, qkv_bias, out_weight, out_bias, up_weight, up_bias, down_weight, down_bias):
    params = tuple((entry.astype(jnp.float32) for entry in (ln1_gain, ln1_bias, ln2_gain, ln2_bias, qkv_weight, qkv_bias, out_weight, out_bias, up_weight, up_bias, down_weight, down_bias)))
    x_all = hidden_in.astype(jnp.float32)

    def whole(x_in, *param_in):
        return forward(x_in, segment_ids, param_in)
    result, pull = jax.vjp(whole, x_all, *params)
    valid = (segment_ids >= 0)[:, None]
    grad_y = jnp.where(valid, cotangent.astype(jnp.float32), jnp.zeros_like(x_all))
    grads = pull(grad_y)
    return (result.astype(jnp.bfloat16), grads[0], grads[1], grads[2], grads[3], grads[4], grads[5], grads[6], grads[7], grads[8], grads[9], grads[10], grads[11], grads[12])
```

```python
import functools

import jax
import jax.numpy as jnp
from jax import lax
from jax.experimental import pallas as pl
from jax.experimental.pallas import tpu as pltpu
from jax.sharding import PartitionSpec as P

D = 768
HEADS = 12
HEAD_DIM = 64
ROTARY = 16
EPS = 1e-05
PAIR = 2 * HEAD_DIM
PAIRS = HEADS // 2
VMEM_BYTES = 56 * 1024 * 1024
F32 = jnp.float32
BF16 = jnp.bfloat16


def positions(segments):
    slot_index = jnp.arange(segments.shape[0], dtype=jnp.int32)
    is_start = jnp.concatenate([jnp.ones((1,), bool), segments[1:] != segments[:-1]])
    seq_start = lax.cummax(jnp.where(is_start, slot_index, jnp.zeros_like(slot_index)), axis=0)
    return slot_index - seq_start


def turn_tables(places):
    half = ROTARY // 2
    length = places.shape[0]
    rates = 10000.0 ** (-(jnp.arange(half, dtype=F32) * 2.0) / ROTARY)
    turned = places.astype(F32)[:, None] * rates[None, :]
    cosine, sine = jnp.cos(turned), jnp.sin(turned)
    rest = HEAD_DIM - ROTARY
    zero_half = jnp.zeros((length, half), F32)
    zeros = jnp.zeros((length, rest), F32)
    keep = jnp.concatenate([cosine, cosine, jnp.ones((length, rest), F32)], -1)
    ahead = jnp.concatenate([-sine, zero_half, zeros], -1)
    behind = jnp.concatenate([zero_half, sine, zeros], -1)
    return tuple(jnp.concatenate([item, item], -1) for item in (keep, ahead, behind))


def contract_rows(left, right):
    return lax.dot_general(left, right, (((0,), (0,)), ((), ())), preferred_element_type=F32)


def across(left, right):
    return lax.dot_general(left, right, (((1,), (1,)), ((), ())), preferred_element_type=F32)


def dot(left, right):
    return jnp.dot(left, right, preferred_element_type=F32)


def attention_kernel(
    rows,
    a1_ref,
    dy_ref,
    wq_ref,
    wk_ref,
    wv_ref,
    bq_ref,
    bk_ref,
    bv_ref,
    wo_ref,
    keep_ref,
    ahead_ref,
    behind_ref,
    seg_col_ref,
    seg_row_ref,
    o_ref,
    dqkv_ref,
    bias_ref,
    dkt_ref,
    dvt_ref,
):
    number = pl.program_id(0)
    length = a1_ref.shape[0]
    half = ROTARY // 2

    @pl.when(number == 0)
    def _():
        row_id = lax.broadcasted_iota(jnp.int32, (length, length), 0)
        col_id = lax.broadcasted_iota(jnp.int32, (length, length), 1)
        readable = (seg_col_ref[...] == seg_row_ref[...]) & (row_id >= col_id)
        bias_ref[...] = jnp.where(readable, 0.0, -1e30)

    keep, ahead, behind = keep_ref[...], ahead_ref[...], behind_ref[...]

    def turn(u):
        return (
            u * keep
            + pltpu.roll(u, PAIR - half, 1) * ahead
            + pltpu.roll(u, half, 1) * behind
        )

    def turn_back(g):
        return (
            g * keep
            + pltpu.roll(g * ahead, half, 1)
            + pltpu.roll(g * behind, PAIR - half, 1)
        )

    a1 = a1_ref[...]
    q = (turn(dot(a1, wq_ref[...]) + bq_ref[...])).astype(BF16)
    q = (q.astype(F32) * 0.125)
    k = (turn(dot(a1, wk_ref[...]) + bk_ref[...])).astype(BF16).astype(F32)
    v = (dot(a1, wv_ref[...]) + bv_ref[...]).astype(BF16).astype(F32)
    do = across(dy_ref[...], wo_ref[...]).astype(BF16).astype(F32)
    lane = lax.broadcasted_iota(jnp.int32, (length, PAIR), 1)
    first = lane < HEAD_DIM
    zero = jnp.zeros_like(q)

    def split(item):
        return (
            jnp.where(first, item, zero).astype(BF16),
            jnp.where(first, zero, item).astype(BF16),
        )

    q_of, k_of, v_of, do_of = split(q), split(k), split(v), split(do)
    qt, kt = jnp.transpose(q).astype(BF16), jnp.transpose(k).astype(BF16)
    vt, dot_t = jnp.transpose(v).astype(BF16), jnp.transpose(do).astype(BF16)
    dkt_ref[...] = jnp.zeros_like(dkt_ref)
    dvt_ref[...] = jnp.zeros_like(dvt_ref)
    dq_parts = []
    for block in range(length // rows):
        lo, hi = block * rows, (block + 1) * rows
        bias = bias_ref[lo:hi, :hi]
        out = None
        dq = None
        for head in range(2):
            h0, h1 = head * HEAD_DIM, (head + 1) * HEAD_DIM
            scores = dot(q_of[head][lo:hi], kt[:, :hi]) + bias
            raised = jnp.exp(scores - jnp.max(scores, -1, keepdims=True))
            weights = raised * (1.0 / jnp.sum(raised, -1, keepdims=True))
            low = weights.astype(BF16)
            part = dot(low, v_of[head][:hi])
            out = part if out is None else out + part
            dvt_ref[h0:h1, :hi] += dot(dot_t[h0:h1, lo:hi], low)
            grad_w = dot(do_of[head][lo:hi], vt[:, :hi])
            prod = weights * grad_w
            centre = jnp.sum(prod, -1, keepdims=True)
            grad_s = (prod - weights * centre).astype(BF16)
            part = dot(grad_s, k_of[head][:hi])
            dq = part if dq is None else dq + part
            dkt_ref[h0:h1, :hi] += dot(qt[h0:h1, lo:hi], grad_s)
        o_ref[lo:hi, :] = out.astype(BF16)
        dq_parts.append(dq * 0.125)
    dq = turn_back(jnp.concatenate(dq_parts, 0))
    dk = turn_back(jnp.transpose(dkt_ref[...]))
    dv = jnp.transpose(dvt_ref[...])
    for index, item in enumerate((dq, dk, dv)):
        spot = pl.multiple_of(index * D + number * PAIR, PAIR)
        dqkv_ref[:, pl.ds(spot, PAIR)] = item.astype(BF16)


def attention(a1, dy, w_qkv, b_qkv, w_out, tables, segments):
    length = a1.shape[0]
    whole = lambda shape: pl.BlockSpec(shape, lambda j: (0, 0))
    column = lambda shift: pl.BlockSpec((D, PAIR), lambda j: (0, shift + j))
    bias = lambda shift: pl.BlockSpec((1, PAIR), lambda j: (0, shift + j))
    b_row = b_qkv.reshape(1, 3 * D)
    return pl.pallas_call(
        functools.partial(attention_kernel, 256),
        grid=(PAIRS,),
        out_shape=(
            jax.ShapeDtypeStruct((length, D), BF16),
            jax.ShapeDtypeStruct((length, 3 * D), BF16),
        ),
        in_specs=[
            whole((length, D)),
            whole((length, D)),
            column(0),
            column(PAIRS),
            column(2 * PAIRS),
            bias(0),
            bias(PAIRS),
            bias(2 * PAIRS),
            pl.BlockSpec((PAIR, D), lambda j: (j, 0)),
            whole((length, PAIR)),
            whole((length, PAIR)),
            whole((length, PAIR)),
            whole((length, 1)),
            whole((1, length)),
        ],
        out_specs=(
            pl.BlockSpec((length, PAIR), lambda j: (0, j)),
            whole((length, 3 * D)),
        ),
        scratch_shapes=[
            pltpu.VMEM((length, length), F32),
            pltpu.VMEM((PAIR, length), F32),
            pltpu.VMEM((PAIR, length), F32),
        ],
        compiler_params=pltpu.CompilerParams(
            dimension_semantics=("arbitrary",), vmem_limit_bytes=VMEM_BYTES
        ),
        cost_estimate=pl.CostEstimate(
            flops=40_000_000_000, bytes_accessed=20_000_000, transcendentals=8_000_000
        ),
    )(
        a1,
        dy,
        w_qkv,
        w_qkv,
        w_qkv,
        b_row,
        b_row,
        b_row,
        w_out,
        *tables,
        segments.reshape(length, 1),
        segments.reshape(1, length),
    )


def feed_kernel(a2_ref, dy_ref, wu_ref, bu_ref, wd_ref, mlp_ref, da2_ref, gu_ref, gd_ref, gb_ref, h_ref, du_ref):
    number = pl.program_id(0)
    length = a2_ref.shape[0]
    step = length // 4

    @pl.when(number == 0)
    def _():
        mlp_ref[...] = jnp.zeros_like(mlp_ref)
        da2_ref[...] = jnp.zeros_like(da2_ref)

    total = None
    for lo in range(0, length, step):
        rows = slice(lo, lo + step)
        u = dot(a2_ref[rows, :], wu_ref[...]) + bu_ref[...]
        area = 0.5 + 0.5 * lax.erf(u * (0.5**0.5))
        h_ref[rows, :] = (u * area).astype(BF16)
        slope = area + u * (jnp.exp(u * u * -0.5) * 0.3989422804014327)
        du = (across(dy_ref[rows, :], wd_ref[...]) * slope).astype(BF16)
        du_ref[rows, :] = du
        part = jnp.sum(du.astype(F32), 0, keepdims=True)
        total = part if total is None else total + part
        mlp_ref[rows, :] += dot(h_ref[rows, :], wd_ref[...])
        da2_ref[rows, :] += across(du, wu_ref[...])
    gb_ref[...] = total
    gu_ref[...] = contract_rows(a2_ref[...], du_ref[...]).astype(gu_ref.dtype)
    gd_ref[...] = contract_rows(h_ref[...], dy_ref[...]).astype(gd_ref.dtype)


def feed(a2, dy, w_up, b_up, w_down):
    length = a2.shape[0]
    width = w_up.shape[1]
    block = 512
    whole = lambda shape: pl.BlockSpec(shape, lambda j: (0, 0))
    return pl.pallas_call(
        feed_kernel,
        grid=(width // block,),
        out_shape=(
            jax.ShapeDtypeStruct((length, D), F32),
            jax.ShapeDtypeStruct((length, D), F32),
            jax.ShapeDtypeStruct((D, width), BF16),
            jax.ShapeDtypeStruct((width, D), BF16),
            jax.ShapeDtypeStruct((1, width), F32),
        ),
        in_specs=[
            whole((length, D)),
            whole((length, D)),
            pl.BlockSpec((D, block), lambda j: (0, j)),
            pl.BlockSpec((1, block), lambda j: (0, j)),
            pl.BlockSpec((block, D), lambda j: (j, 0)),
        ],
        out_specs=(
            whole((length, D)),
            whole((length, D)),
            pl.BlockSpec((D, block), lambda j: (0, j)),
            pl.BlockSpec((block, D), lambda j: (j, 0)),
            pl.BlockSpec((1, block), lambda j: (0, j)),
        ),
        scratch_shapes=[
            pltpu.VMEM((length, block), BF16),
            pltpu.VMEM((length, block), BF16),
        ],
        compiler_params=pltpu.CompilerParams(
            dimension_semantics=("arbitrary",), vmem_limit_bytes=VMEM_BYTES
        ),
        cost_estimate=pl.CostEstimate(
            flops=29_000_000_000, bytes_accessed=30_000_000, transcendentals=6_000_000
        ),
    )(a2, dy, w_up, b_up.reshape(1, width), w_down)


def local(
    hidden_in,
    segment_ids,
    cotangent,
    ln1_gain,
    ln1_bias,
    ln2_gain,
    ln2_bias,
    qkv_weight,
    qkv_bias,
    out_weight,
    out_bias,
    up_weight,
    up_bias,
    down_weight,
    down_bias,
):
    gather = lambda item: lax.all_gather(item, "shard", axis=0, tiled=True)
    vectors = (ln1_gain, ln1_bias, ln2_gain, ln2_bias, qkv_bias, out_bias, up_bias, down_bias)
    sizes = [item.shape[0] for item in vectors]
    offsets = [sum(sizes[:index]) for index in range(len(sizes))]
    group = lax.axis_size("shard")
    packed = gather(jnp.concatenate(vectors)).reshape(group, sum(sizes)).astype(F32)
    gain_one, bias_one, gain_two, bias_two, b_qkv, b_out, b_up, b_down = tuple(
        packed[:, offset : offset + size].reshape(-1) for offset, size in zip(offsets, sizes)
    )
    w_out = gather(out_weight)
    w_qkv = gather(qkv_weight)
    up_weight, down_weight, w_qkv, w_out = lax.optimization_barrier(
        (up_weight, down_weight, w_qkv, w_out)
    )
    w_up = gather(up_weight)
    w_down = gather(down_weight)

    x = hidden_in.astype(F32)
    center = x - jnp.mean(x, -1, keepdims=True)
    scale = lax.rsqrt(jnp.mean(center * center, -1, keepdims=True) + EPS)
    unit = center * scale
    a1 = (unit * gain_one + bias_one).astype(BF16)
    a2 = (unit * gain_two + bias_two).astype(BF16)
    dy = jnp.where((segment_ids >= 0)[:, None], cotangent, jnp.zeros_like(cotangent))
    dy_float = dy.astype(F32)
    tables = turn_tables(positions(segment_ids))

    o, dqkv = attention(a1, dy, w_qkv, b_qkv, w_out, tables, segment_ids)
    scatter = lambda item: lax.psum_scatter(item, "shard", scatter_dimension=0, tiled=True)
    g_qkv = lax.psum(scatter(contract_rows(a1, dqkv).astype(BF16)), "rep")
    g_out = lax.psum(scatter(contract_rows(o, dy).astype(BF16)), "rep")
    mlp, da2, g_up, g_down, g_up_bias = feed(a2, dy, w_up, b_up, w_down)
    g_up, g_down, g_qkv, g_out = lax.optimization_barrier((g_up, g_down, g_qkv, g_out))
    g_up = lax.psum(scatter(g_up), "rep")
    g_down = lax.psum(scatter(g_down), "rep")

    da1 = across(dqkv, w_qkv)
    mixed = (x + (dot(o, w_out) + b_out) + (mlp + b_down)).astype(BF16)
    d_unit = da1 * gain_one + da2 * gain_two
    d_x = scale * (
        d_unit
        - jnp.mean(d_unit, -1, keepdims=True)
        - unit * jnp.mean(d_unit * unit, -1, keepdims=True)
    )
    input_grad = dy_float + d_x
    sum_dy = jnp.sum(dy_float, 0)
    grads = (
        jnp.sum(da1 * unit, 0),
        jnp.sum(da1, 0),
        jnp.sum(da2 * unit, 0),
        jnp.sum(da2, 0),
        jnp.sum(dqkv.astype(F32), 0),
        sum_dy,
        g_up_bias.reshape(-1),
        sum_dy,
    )
    small = jnp.concatenate([item.reshape(group, -1) for item in grads], 1).reshape(-1)
    small = lax.psum(small, ("rep", "shard")).reshape(group, -1)
    mine = lax.dynamic_index_in_dim(small, lax.axis_index("shard"), 0, keepdims=False)
    own = tuple(mine[offset : offset + size] for offset, size in zip(offsets, sizes))
    return (
        mixed,
        input_grad,
        own[0],
        own[1],
        own[2],
        own[3],
        g_qkv.astype(F32),
        own[4],
        g_out.astype(F32),
        own[5],
        g_up.astype(F32),
        own[6],
        g_down.astype(F32),
        own[7],
    )


def solution(mesh):
    tokens = P(("rep", "shard"), None)
    row, matrix = P("shard"), P("shard", None)
    return jax.shard_map(
        local,
        mesh=mesh,
        in_specs=(tokens, P(("rep", "shard")), tokens, row, row, row, row)
        + (matrix, row) * 4,
        out_specs=(tokens, tokens, row, row, row, row) + (matrix, row) * 4,
        check_vma=False,
    )
```

```python
import functools

import jax
import jax.numpy as jnp
from jax import lax
from jax.experimental import pallas as pl
from jax.experimental.pallas import tpu as pltpu
from jax.sharding import PartitionSpec as P

D = 768
HEADS = 12
HEAD_DIM = 64
ROTARY = 16
EPS = 1e-05
PAIR = 2 * HEAD_DIM
PAIRS = HEADS // 2
VMEM_BYTES = 56 * 1024 * 1024
F32 = jnp.float32
BF16 = jnp.bfloat16


def positions(segments):
    slot_index = jnp.arange(segments.shape[0], dtype=jnp.int32)
    is_start = jnp.concatenate([jnp.ones((1,), bool), segments[1:] != segments[:-1]])
    seq_start = lax.cummax(jnp.where(is_start, slot_index, jnp.zeros_like(slot_index)), axis=0)
    return slot_index - seq_start


def turn_tables(places):
    half = ROTARY // 2
    length = places.shape[0]
    rates = 10000.0 ** (-(jnp.arange(half, dtype=F32) * 2.0) / ROTARY)
    turned = places.astype(F32)[:, None] * rates[None, :]
    cosine, sine = jnp.cos(turned), jnp.sin(turned)
    rest = HEAD_DIM - ROTARY
    zero_half = jnp.zeros((length, half), F32)
    zeros = jnp.zeros((length, rest), F32)
    keep = jnp.concatenate([cosine, cosine, jnp.ones((length, rest), F32)], -1)
    ahead = jnp.concatenate([-sine, zero_half, zeros], -1)
    behind = jnp.concatenate([zero_half, sine, zeros], -1)
    return tuple(jnp.concatenate([item, item], -1) for item in (keep, ahead, behind))


def contract_rows(left, right):
    return lax.dot_general(left, right, (((0,), (0,)), ((), ())), preferred_element_type=F32)


def across(left, right):
    return lax.dot_general(left, right, (((1,), (1,)), ((), ())), preferred_element_type=F32)


def dot(left, right):
    return jnp.dot(left, right, preferred_element_type=F32)


def attention_kernel(
    rows,
    a1_ref,
    dy_ref,
    wq_ref,
    wk_ref,
    wv_ref,
    bq_ref,
    bk_ref,
    bv_ref,
    wo_ref,
    keep_ref,
    ahead_ref,
    behind_ref,
    seg_col_ref,
    seg_row_ref,
    o_ref,
    dqkv_ref,
    bias_ref,
    dkt_ref,
    dvt_ref,
):
    number = pl.program_id(0)
    length = a1_ref.shape[0]
    half = ROTARY // 2

    @pl.when(number == 0)
    def _():
        row_id = lax.broadcasted_iota(jnp.int32, (length, length), 0)
        col_id = lax.broadcasted_iota(jnp.int32, (length, length), 1)
        readable = (seg_col_ref[...] == seg_row_ref[...]) & (row_id >= col_id)
        bias_ref[...] = jnp.where(readable, 0.0, -1e30)

    keep, ahead, behind = keep_ref[...], ahead_ref[...], behind_ref[...]

    def turn(u):
        return (
            u * keep
            + pltpu.roll(u, PAIR - half, 1) * ahead
            + pltpu.roll(u, half, 1) * behind
        )

    def turn_back(g):
        return (
            g * keep
            + pltpu.roll(g * ahead, half, 1)
            + pltpu.roll(g * behind, PAIR - half, 1)
        )

    a1 = a1_ref[...]
    q = (turn(dot(a1, wq_ref[...]) + bq_ref[...])).astype(BF16)
    q = (q.astype(F32) * 0.125)
    k = (turn(dot(a1, wk_ref[...]) + bk_ref[...])).astype(BF16).astype(F32)
    v = (dot(a1, wv_ref[...]) + bv_ref[...]).astype(BF16).astype(F32)
    do = across(dy_ref[...], wo_ref[...]).astype(BF16).astype(F32)
    lane = lax.broadcasted_iota(jnp.int32, (length, PAIR), 1)
    first = lane < HEAD_DIM
    zero = jnp.zeros_like(q)

    def split(item):
        return (
            jnp.where(first, item, zero).astype(BF16),
            jnp.where(first, zero, item).astype(BF16),
        )

    q_of, k_of, v_of, do_of = split(q), split(k), split(v), split(do)
    qt, kt = jnp.transpose(q).astype(BF16), jnp.transpose(k).astype(BF16)
    vt, dot_t = jnp.transpose(v).astype(BF16), jnp.transpose(do).astype(BF16)
    dkt_ref[...] = jnp.zeros_like(dkt_ref)
    dvt_ref[...] = jnp.zeros_like(dvt_ref)
    dq_parts = []
    for block in range(length // rows):
        lo, hi = block * rows, (block + 1) * rows
        bias = bias_ref[lo:hi, :hi]
        out = None
        dq = None
        for head in range(2):
            h0, h1 = head * HEAD_DIM, (head + 1) * HEAD_DIM
            scores = dot(q_of[head][lo:hi], kt[:, :hi]) + bias
            raised = jnp.exp(scores - jnp.max(scores, -1, keepdims=True))
            weights = raised * (1.0 / jnp.sum(raised, -1, keepdims=True))
            low = weights.astype(BF16)
            part = dot(low, v_of[head][:hi])
            out = part if out is None else out + part
            dvt_ref[h0:h1, :hi] += dot(dot_t[h0:h1, lo:hi], low)
            grad_w = dot(do_of[head][lo:hi], vt[:, :hi])
            prod = weights * grad_w
            centre = jnp.sum(prod, -1, keepdims=True)
            grad_s = (prod - weights * centre).astype(BF16)
            part = dot(grad_s, k_of[head][:hi])
            dq = part if dq is None else dq + part
            dkt_ref[h0:h1, :hi] += dot(qt[h0:h1, lo:hi], grad_s)
        o_ref[lo:hi, :] = out.astype(BF16)
        dq_parts.append(dq * 0.125)
    dq = turn_back(jnp.concatenate(dq_parts, 0))
    dk = turn_back(jnp.transpose(dkt_ref[...]))
    dv = jnp.transpose(dvt_ref[...])
    for index, item in enumerate((dq, dk, dv)):
        spot = pl.multiple_of(index * D + number * PAIR, PAIR)
        dqkv_ref[:, pl.ds(spot, PAIR)] = item.astype(BF16)


def attention(a1, dy, w_attn, b_qkv, tables, segments):
    length = a1.shape[0]
    whole = lambda shape: pl.BlockSpec(shape, lambda j: (0, 0))
    column = lambda shift: pl.BlockSpec((D, PAIR), lambda j: (0, shift + j))
    bias = lambda shift: pl.BlockSpec((1, PAIR), lambda j: (0, shift + j))
    b_row = b_qkv.reshape(1, 3 * D)
    return pl.pallas_call(
        functools.partial(attention_kernel, 256),
        grid=(PAIRS,),
        out_shape=(
            jax.ShapeDtypeStruct((length, D), BF16),
            jax.ShapeDtypeStruct((length, 3 * D), BF16),
        ),
        in_specs=[
            whole((length, D)),
            whole((length, D)),
            column(0),
            column(PAIRS),
            column(2 * PAIRS),
            bias(0),
            bias(PAIRS),
            bias(2 * PAIRS),
            pl.BlockSpec((PAIR, D), lambda j: (j, 3)),
            whole((length, PAIR)),
            whole((length, PAIR)),
            whole((length, PAIR)),
            whole((length, 1)),
            whole((1, length)),
        ],
        out_specs=(
            pl.BlockSpec((length, PAIR), lambda j: (0, j)),
            whole((length, 3 * D)),
        ),
        scratch_shapes=[
            pltpu.VMEM((length, length), F32),
            pltpu.VMEM((PAIR, length), F32),
            pltpu.VMEM((PAIR, length), F32),
        ],
        compiler_params=pltpu.CompilerParams(
            dimension_semantics=("arbitrary",), vmem_limit_bytes=VMEM_BYTES
        ),
        cost_estimate=pl.CostEstimate(
            flops=40_000_000_000, bytes_accessed=20_000_000, transcendentals=8_000_000
        ),
    )(
        a1,
        dy,
        w_attn,
        w_attn,
        w_attn,
        b_row,
        b_row,
        b_row,
        w_attn,
        *tables,
        segments.reshape(length, 1),
        segments.reshape(1, length),
    )


def feed_kernel(
    a2_ref, dy_ref, wu_ref, bu_ref, wd_ref, mlp_ref, da2_ref, grad_ref, gb_ref, h_ref, du_ref
):
    number = pl.program_id(0)
    length = a2_ref.shape[0]
    group, owned, block = wu_ref.shape
    parts = block // wd_ref.shape[1]
    step = length // 4

    @pl.when(number == 0)
    def _():
        mlp_ref[...] = jnp.zeros_like(mlp_ref)
        da2_ref[...] = jnp.zeros_like(da2_ref)

    wu = wu_ref[...].reshape(D, block)
    wd = wd_ref[...].reshape(block, D)
    total = None
    for lo in range(0, length, step):
        rows = slice(lo, lo + step)
        u = dot(a2_ref[rows, :], wu) + bu_ref[...]
        area = 0.5 + 0.5 * lax.erf(u * (0.5**0.5))
        h_ref[rows, :] = (u * area).astype(BF16)
        slope = area + u * (jnp.exp(u * u * -0.5) * 0.3989422804014327)
        du = (across(dy_ref[rows, :], wd) * slope).astype(BF16)
        du_ref[rows, :] = du
        part = jnp.sum(du.astype(F32), 0, keepdims=True)
        total = part if total is None else total + part
        mlp_ref[rows, :] += dot(h_ref[rows, :], wd)
        da2_ref[rows, :] += across(du, wu)
    gb_ref[...] = total
    gu = contract_rows(a2_ref[...], du_ref[...]).astype(BF16)
    spot = pl.multiple_of(number * owned, owned)
    grad_ref[:, pl.ds(spot, owned), :] = gu.reshape(group, owned, block)
    gd = contract_rows(h_ref[...], dy_ref[...]).astype(BF16)
    held = wd_ref.shape[1]
    lead = grad_ref.shape[1] - held
    grad_ref[pl.ds(number * parts, parts), lead:, :] = gd.reshape(parts, held, D)


def feed(a2, dy, w_feed, b_up):
    length = a2.shape[0]
    group = w_feed.shape[0]
    owned = D // group
    width = b_up.shape[0]
    held = width // group
    block = D
    parts = block // held
    chunks = width // block
    whole = lambda shape: pl.BlockSpec(shape, lambda j: (0, 0))
    return pl.pallas_call(
        feed_kernel,
        grid=(chunks,),
        out_shape=(
            jax.ShapeDtypeStruct((length, D), F32),
            jax.ShapeDtypeStruct((length, D), F32),
            jax.ShapeDtypeStruct(w_feed.shape, BF16),
            jax.ShapeDtypeStruct((1, width), F32),
        ),
        in_specs=[
            whole((length, D)),
            whole((length, D)),
            pl.BlockSpec((group, owned, block), lambda j: (0, j, 0)),
            pl.BlockSpec((1, block), lambda j: (0, j)),
            pl.BlockSpec((parts, held, D), lambda j: (j, chunks * owned // held, 0)),
        ],
        out_specs=(
            whole((length, D)),
            whole((length, D)),
            pl.BlockSpec(w_feed.shape, lambda j: (0, 0, 0)),
            pl.BlockSpec((1, block), lambda j: (0, j)),
        ),
        scratch_shapes=[
            pltpu.VMEM((length, block), BF16),
            pltpu.VMEM((length, block), BF16),
        ],
        compiler_params=pltpu.CompilerParams(
            dimension_semantics=("arbitrary",), vmem_limit_bytes=VMEM_BYTES
        ),
        cost_estimate=pl.CostEstimate(
            flops=29_000_000_000, bytes_accessed=30_000_000, transcendentals=6_000_000
        ),
    )(a2, dy, w_feed, b_up.reshape(1, width), w_feed)


def scatter_owner(grad):
    flat = grad.reshape(-1, grad.shape[-1])
    return lax.psum_scatter(flat, "shard", scatter_dimension=0, tiled=True)


def sum_copies(grads):
    return lax.psum(grads, "rep")


def local(
    hidden_in,
    segment_ids,
    cotangent,
    ln1_gain,
    ln1_bias,
    ln2_gain,
    ln2_bias,
    qkv_weight,
    qkv_bias,
    out_weight,
    out_bias,
    up_weight,
    up_bias,
    down_weight,
    down_bias,
):
    gather = lambda item: lax.all_gather(item, "shard", axis=0, tiled=True)
    vectors = (ln1_gain, ln1_bias, ln2_gain, ln2_bias, qkv_bias, out_bias, up_bias, down_bias)
    sizes = [item.shape[0] for item in vectors]
    offsets = [sum(sizes[:index]) for index in range(len(sizes))]
    group = lax.axis_size("shard")
    packed = gather(jnp.concatenate(vectors)).reshape(group, sum(sizes)).astype(F32)
    gain_one, bias_one, gain_two, bias_two, b_qkv, b_out, b_up, b_down = tuple(
        packed[:, offset : offset + size].reshape(-1) for offset, size in zip(offsets, sizes)
    )
    owned, width = up_weight.shape
    chunks = width // D
    w_attn = gather(jnp.concatenate([qkv_weight, out_weight], 1))
    stacked = jnp.concatenate(
        [up_weight[:, index * D : (index + 1) * D] for index in range(chunks)] + [down_weight], 0
    )
    stacked, w_attn = lax.optimization_barrier((stacked, w_attn))
    w_feed = lax.all_gather(stacked, "shard", axis=0, tiled=False)

    x = hidden_in.astype(F32)
    center = x - jnp.mean(x, -1, keepdims=True)
    scale = lax.rsqrt(jnp.mean(center * center, -1, keepdims=True) + EPS)
    unit = center * scale
    a1 = (unit * gain_one + bias_one).astype(BF16)
    a2 = (unit * gain_two + bias_two).astype(BF16)
    dy = jnp.where((segment_ids >= 0)[:, None], cotangent, jnp.zeros_like(cotangent))
    dy_float = dy.astype(F32)
    tables = turn_tables(positions(segment_ids))

    o, dqkv = attention(a1, dy, w_attn, b_qkv, tables, segment_ids)
    g_attn = jnp.concatenate([contract_rows(a1, dqkv), contract_rows(o, dy)], 1).astype(BF16)
    g_attn, w_feed = lax.optimization_barrier((g_attn, w_feed))
    g_attn = scatter_owner(g_attn.reshape(group, owned, -1))
    mlp, da2, g_feed, g_up_bias = feed(a2, dy, w_feed, b_up)
    g_feed, g_attn = lax.optimization_barrier((g_feed, g_attn))
    g_feed = scatter_owner(g_feed)
    g_attn, g_feed = sum_copies((g_attn, g_feed))
    w_qkv, w_out = w_attn[:, : 3 * D], w_attn[:, 3 * D :]
    lead = chunks * owned
    g_up = jnp.concatenate(
        [g_feed[index * owned : (index + 1) * owned] for index in range(chunks)], 1
    )

    da1 = across(dqkv, w_qkv)
    mixed = (x + (dot(o, w_out) + b_out) + (mlp + b_down)).astype(BF16)
    d_unit = da1 * gain_one + da2 * gain_two
    d_x = scale * (
        d_unit
        - jnp.mean(d_unit, -1, keepdims=True)
        - unit * jnp.mean(d_unit * unit, -1, keepdims=True)
    )
    input_grad = dy_float + d_x
    sum_dy = jnp.sum(dy_float, 0)
    grads = (
        jnp.sum(da1 * unit, 0),
        jnp.sum(da1, 0),
        jnp.sum(da2 * unit, 0),
        jnp.sum(da2, 0),
        jnp.sum(dqkv.astype(F32), 0),
        sum_dy,
        g_up_bias.reshape(-1),
        sum_dy,
    )
    small = jnp.concatenate([item.reshape(group, -1) for item in grads], 1).reshape(-1)
    small = lax.psum(small, ("rep", "shard")).reshape(group, -1)
    mine = lax.dynamic_index_in_dim(small, lax.axis_index("shard"), 0, keepdims=False)
    own = tuple(mine[offset : offset + size] for offset, size in zip(offsets, sizes))
    return (
        mixed,
        input_grad,
        own[0],
        own[1],
        own[2],
        own[3],
        g_attn[:, : 3 * D].astype(F32),
        own[4],
        g_attn[:, 3 * D :].astype(F32),
        own[5],
        g_up.astype(F32),
        own[6],
        g_feed[lead:].astype(F32),
        own[7],
    )


def solution(mesh):
    tokens = P(("rep", "shard"), None)
    row, matrix = P("shard"), P("shard", None)
    return jax.shard_map(
        local,
        mesh=mesh,
        in_specs=(tokens, P(("rep", "shard")), tokens, row, row, row, row)
        + (matrix, row) * 4,
        out_specs=(tokens, tokens, row, row, row, row) + (matrix, row) * 4,
        check_vma=False,
    )
```
